512 devices in a mesh: lat: 16 (over x, y_hi), lon: 32 (over y_lo, z, core).
Axes of the slice: x: 4, y: 8 (y_hi: 4, y_lo: 2; y = y_hi * 2 + y_lo), z: 8, core: 2. Of those that a mesh axis runs over, the one named last changes fastest.
Arguments:
- level_tokens: bfloat16 [13, 96, 384, 512], P(None, 'lat', 'lon'), may hold values from -6 to 6
- hidden_probe_match_matrix: bfloat16 [3, 16, 512], replicated, may hold values from -0.5 to 0.5
- value_weight: bfloat16 [512, 512], P('lon'), may hold values from -0.25 to 0.25
- pool_out_weight: bfloat16 [512, 512], P('lon'), may hold values from -0.25 to 0.25
- latent_base: bfloat16 [3, 512], replicated, may hold values from -5 to 5
- norm_gain: float32 [512], replicated, may hold values from 0.25 to 1.75
- qkv_weight: bfloat16 [512, 1536], P('lon'), may hold values from -0.25 to 0.25
- attn_out_weight: bfloat16 [512, 512], P('lon'), may hold values from -0.25 to 0.25
- region_ids: int32 [96, 384], P('lat', 'lon'), may hold values from 0 to 3, as said below
Outputs:
- latent_out: bfloat16 [3, 96, 384, 512], P(None, 'lat', 'lon')
The draws below stay inside these ranges and needn't reach their ends.
Inputs may be any that keep to these rules, and one draw needn't show every extreme that they name: region_ids is constant on each block of 3 rows by 6 columns aligned to multiples of these sizes.
All inputs are finite; a program needn't handle non-finite values.
Results may differ from the reference program's by a relative error of at most 0.019.
Values may be sent and summed in bfloat16 or wider, within the bound.
No kernel may reach another device: no remote copies, remote signals or barrier semaphores. Data moves between devices by JAX's collectives and lax.ppermute only.
A program may use at most 64 MiB of HBM per device.

```python
import jax
import jax.numpy as jnp
from jax import lax

D = 512
HEADS = 8
POOLING_HEADS = 16
LEVELS = 13
LATENTS = 3
WIN_LAT = 6
WIN_LON = 12
NLAT = 96
NLON = 384


def draw_region_ids(key, part):
    key = jax.random.fold_in(key, 7)
    block_rows = NLAT // (WIN_LAT // 2)
    block_cols = NLON // (WIN_LON // 2)
    blocks = jax.random.randint(key, (block_rows, block_cols), 0, 4, dtype=jnp.int32)
    row_index = jnp.arange(block_rows, dtype=jnp.int32)[:, None]
    col_index = jnp.arange(block_cols, dtype=jnp.int32)[None, :]
    first_row = row_index == 0
    blocks = jnp.where(first_row & (col_index == 0), 0, blocks)
    blocks = jnp.where(first_row & (col_index == 1), 3, blocks)
    cells = jnp.repeat(blocks, WIN_LAT // 2, axis=0)
    cells = jnp.repeat(cells, WIN_LON // 2, axis=1)
    return cells.astype(jnp.int32)


def block_levels(own_key, dims, split, least, largest):
    def one(dim, parts):
        draws = jax.random.uniform(jax.random.fold_in(jax.random.fold_in(own_key, 6), dim), (parts,), jnp.float32, least / len(split), largest / len(split))
        return jnp.repeat(jnp.exp(draws), dims[dim] // parts).reshape((-1,) + (1,) * (len(dims) - dim - 1))

    loudness = one(*split[0])
    for cut in split[1:]:
        loudness = loudness * one(*cut)
    return loudness


def bell_draw(stream_key, extent, scale, most, pieces=(), held_as=jnp.bfloat16):
    array = scale * jax.random.normal(stream_key, extent, jnp.float32)
    if pieces:
        array = array * block_levels(stream_key, extent, pieces, -0.22, 0.18)
    return jnp.clip(array, -most, most).astype(held_as)


def setup_inputs(seed: int = 0) -> dict:
    splits = jax.random.split(jax.random.key(seed), 10)
    level_tokens = bell_draw(splits[0], (LEVELS, NLAT, NLON, D), 1.0, 6.0, ((1, 16), (2, 32)))
    hidden_probe_match_matrix = bell_draw(splits[1], (LATENTS, POOLING_HEADS, D), (D // 4) ** -0.5, 0.5)
    value_weight = bell_draw(splits[2], (D, D), D ** -0.5, 0.25, ((0, 32),))
    pool_out_weight = bell_draw(splits[3], (D, D), D ** -0.5, 0.25, ((0, 32),))
    latent_base = bell_draw(splits[4], (LATENTS, D), 1.0, 5.0)
    norm_gain = jnp.clip(1.0 + 0.15 * jax.random.normal(splits[5], (D,), jnp.float32), 0.25, 1.75)
    qkv_weight = bell_draw(splits[6], (D, 3 * D), D ** -0.5, 0.25, ((0, 32),))
    attn_out_weight = bell_draw(splits[7], (D, D), D ** -0.5, 0.25, ((0, 32),))
    region_ids = draw_region_ids(jax.random.fold_in(splits[9], 71), 0)
    return dict(level_tokens=level_tokens, hidden_probe_match_matrix=hidden_probe_match_matrix, value_weight=value_weight, pool_out_weight=pool_out_weight, latent_base=latent_base, norm_gain=norm_gain, qkv_weight=qkv_weight, attn_out_weight=attn_out_weight, region_ids=region_ids)


STABILIZER_TINY = 1e-05

def layer_norm(latent, norm_gain):
    padded_zonal_band = latent.astype(jnp.float32)
    mean_val = lax.optimization_barrier(jnp.mean(padded_zonal_band, axis=-1, keepdims=True))
    centred = padded_zonal_band - mean_val
    variance = lax.optimization_barrier(jnp.mean(centred * centred, axis=-1, keepdims=True))
    return (centred * lax.rsqrt(variance + STABILIZER_TINY) * norm_gain).astype(jnp.bfloat16)

def attend(projected, levels, row_count, col_count, labels, head_count):
    model_width = projected.shape[-1] // 3
    head_dim = model_width // head_count
    lat_win = row_count // WIN_LAT
    lon_win = col_count // WIN_LON
    window_len = levels * WIN_LAT * WIN_LON
    split_up = projected.reshape(levels, lat_win, WIN_LAT, lon_win, WIN_LON, 3, head_count, head_dim)
    split_up = jnp.transpose(split_up, (5, 1, 3, 6, 0, 2, 4, 7))
    split_up = split_up.reshape(3, lat_win * lon_win, head_count, window_len, head_dim)
    queries = split_up[0].astype(jnp.float32)
    keys_all = split_up[1].astype(jnp.float32)
    value_all = split_up[2].astype(jnp.float32)
    summary_logits = jnp.einsum('whad,whbd->whab', queries, keys_all) / head_dim ** 0.5
    grouped = labels.reshape(lat_win, WIN_LAT, lon_win, WIN_LON).transpose(0, 2, 1, 3)
    grouped = grouped.reshape(lat_win * lon_win, 1, WIN_LAT * WIN_LON)
    grouped = jnp.broadcast_to(grouped, (lat_win * lon_win, levels, WIN_LAT * WIN_LON))
    grouped = grouped.reshape(lat_win * lon_win, window_len)
    allowed = grouped[:, :, None] == grouped[:, None, :]
    summary_logits = jnp.where(allowed[:, None], summary_logits, -1e+30)
    weights = jax.nn.softmax(summary_logits, axis=-1).astype(jnp.bfloat16)
    attended = jnp.einsum('whab,whbd->whad', weights.astype(jnp.float32), value_all).astype(jnp.bfloat16)
    attended = attended.reshape(lat_win, lon_win, head_count, levels, WIN_LAT, WIN_LON, head_dim)
    attended = jnp.transpose(attended, (3, 0, 4, 1, 5, 2, 6))
    return attended.reshape(levels * row_count * col_count, model_width)

def pool_row(isobar_token_matrix, hidden_probe_match_matrix, value_weight, pool_out_weight, latent_base):
    model_width = isobar_token_matrix.shape[-1]
    head_count = hidden_probe_match_matrix.shape[1]
    padded_zonal_band = isobar_token_matrix.astype(jnp.float32)
    summary_logits = jnp.einsum('lep,qdp->qdel', padded_zonal_band, hidden_probe_match_matrix.astype(jnp.float32))
    weights = jax.nn.softmax(summary_logits, axis=-1).astype(jnp.bfloat16)
    pooled = jnp.einsum('mhpl,lpd->mhpd', weights.astype(jnp.float32), padded_zonal_band).astype(jnp.bfloat16)
    per_head = value_weight.astype(jnp.float32).reshape(model_width, head_count, model_width // head_count)
    pool_values = jnp.einsum('mhpd,dhe->mphe', pooled.astype(jnp.float32), per_head)
    pool_values = pool_values.reshape(pool_values.shape[0], pool_values.shape[1], model_width).astype(jnp.bfloat16)
    mixed_sum = jnp.einsum('mpd,de->mpe', pool_values.astype(jnp.float32), pool_out_weight.astype(jnp.float32))
    return (latent_base.astype(jnp.float32)[:, None, :] + mixed_sum).astype(jnp.bfloat16)

def reference(level_tokens, hidden_probe_match_matrix, value_weight, pool_out_weight, latent_base, norm_gain, qkv_weight, attn_out_weight, region_ids):
    lat_rows = level_tokens.shape[1]
    lon_cols = level_tokens.shape[2]
    model_width = level_tokens.shape[3]

    def one_row(row_index):
        isobar_token_matrix = lax.dynamic_index_in_dim(level_tokens, row_index, 1, keepdims=False)
        return pool_row(isobar_token_matrix, hidden_probe_match_matrix, value_weight, pool_out_weight, latent_base)
    pooled_rows = lax.map(one_row, jnp.arange(lat_rows, dtype=jnp.int32))
    latent = jnp.moveaxis(pooled_rows, 0, 1)
    normed = layer_norm(latent, norm_gain)
    half_lat = WIN_LAT // 2
    half_longitude = WIN_LON // 2
    shifted = jnp.roll(normed, (-half_lat, -half_longitude), axis=(1, 2))
    wrapped_longitude = (jnp.arange(lat_rows) >= lat_rows - half_lat).astype(jnp.int32)
    labels_all = region_ids * 2 + wrapped_longitude[:, None]
    band_count = lat_rows // WIN_LAT

    def one_band(band_index):
        first_row = band_index * WIN_LAT
        lat_band = lax.dynamic_slice_in_dim(shifted, first_row, WIN_LAT, 1)
        label_band = lax.dynamic_slice_in_dim(labels_all, first_row, WIN_LAT, 0)
        projected = jnp.dot(lat_band.reshape(-1, model_width), qkv_weight, preferred_element_type=jnp.float32).astype(jnp.bfloat16)
        attended = attend(projected, LATENTS, WIN_LAT, lon_cols, label_band, HEADS)
        attn_proj = jnp.dot(attended, attn_out_weight, preferred_element_type=jnp.float32).astype(jnp.bfloat16)
        return attn_proj.reshape(LATENTS, WIN_LAT, lon_cols, model_width)
    banded = lax.map(one_band, jnp.arange(band_count, dtype=jnp.int32))
    attn_proj = jnp.moveaxis(banded, 0, 1).reshape(LATENTS, lat_rows, lon_cols, model_width)
    attn_proj = jnp.roll(attn_proj, (half_lat, half_longitude), axis=(1, 2))
    return (latent.astype(jnp.float32) + attn_proj.astype(jnp.float32)).astype(jnp.bfloat16)
```

```python
import functools

import jax
import jax.numpy as jnp
from jax import lax
from jax.experimental import pallas as pl
from jax.experimental.pallas import tpu as pltpu
from jax.sharding import PartitionSpec as P

HEADS = 8
LATENTS = 3
WIN_LAT = 6
WIN_LON = 12
HALF_LAT = WIN_LAT // 2
HALF_LON = WIN_LON // 2
CELLS = HALF_LAT * HALF_LON
PADDED = 80
LAT_RING = 4
STABILIZER_TINY = 1e-05
BOTH = ("lat", "lon")


def pairs(source_of, lat_count, lon_count):
    route = []
    for i in range(lat_count):
        for j in range(lon_count):
            si, sj = source_of(i, j)
            source = (si % lat_count) * lon_count + sj % lon_count
            route.append((source, i * lon_count + j))
    return route


def fetch(block, source_of):
    route = pairs(source_of, lax.axis_size("lat"), lax.axis_size("lon"))
    return lax.ppermute(block, BOTH, route)


def give_back(block, source_of):
    route = pairs(source_of, lax.axis_size("lat"), lax.axis_size("lon"))
    return lax.ppermute(block, BOTH, [(b, a) for a, b in route])


def band_of(j):
    return 1 if j % 2 == 0 else -1


def beside(i, j):
    return i, j + 1


def along(i, j):
    return i + band_of(j), j


def across(i, j):
    return i + band_of(j), j + 1


def slice_step(dx, dy):
    def source_of(i, j):
        x, y = i // LAT_RING, i % LAT_RING
        step = dy * band_of(j)
        return ((x + dx) % LAT_RING) * LAT_RING + (y + step) % LAT_RING, j

    return source_of


SLICE_STEPS = ((2, slice_step(0, 1)), (1, slice_step(1, 0)), (3, slice_step(-1, 0)))


def other_core(i, j):
    return i, j + 1 if j % 2 == 0 else j - 1


def window_kernel(
    heads,
    pool_heads,
    place,
    tokens,
    probe,
    own_slices,
    other_slices,
    base,
    gain,
    out,
    weights,
    values,
):
    level_count, cells, width = tokens.shape
    latents = base.shape[0]
    shares = own_slices.shape[0]
    columns = own_slices.shape[2]
    f32 = jnp.float32
    bf16 = jnp.bfloat16
    quad, core = place[0], place[1]
    shifts = (0,) + tuple(step for step, _ in SLICE_STEPS)
    for ref, side in ((own_slices, core), (other_slices, 1 - core)):
        for s in range(shares):
            start = (lax.rem(quad + shifts[s], shares) * 2 + side) * columns
            weights[:, pl.ds(pl.multiple_of(start, 128), columns)] = ref[s]

    x = tokens[...].reshape(level_count * cells, width)
    scores = lax.dot_general(x, probe[...], (((1,), (1,)), ((), ())), preferred_element_type=f32)
    scores = scores.reshape(level_count, cells, latents * pool_heads)
    scores = jnp.exp(scores - jnp.max(scores, axis=0, keepdims=True))
    mix = scores / jnp.sum(scores, axis=0, keepdims=True)
    mix = mix.astype(bf16).reshape(level_count * cells, latents * pool_heads)
    values[...] = jnp.dot(x, weights[:, :width], preferred_element_type=f32)
    span = width // pool_heads
    head_of = lax.broadcasted_iota(jnp.int32, (latents * pool_heads, width), 1) // span
    row_of = lax.broadcasted_iota(jnp.int32, (latents * pool_heads, width), 0)
    pooled = []
    for m in range(latents):
        spread = jnp.where(row_of == head_of + m * pool_heads, 1.0, 0.0).astype(bf16)
        share = jnp.dot(mix, spread, preferred_element_type=f32) * values[...]
        pooled.append(jnp.sum(share.reshape(level_count, cells, width), axis=0).astype(bf16))
    pooled = jnp.concatenate(pooled, axis=0)
    latent = jnp.dot(pooled, weights[:, width : 2 * width], preferred_element_type=f32)
    base_rows = jnp.broadcast_to(base[...].astype(f32)[:, None, :], (latents, cells, width))
    latent = (latent + base_rows.reshape(latents * cells, width)).astype(bf16)

    full = latent.astype(f32)
    centred = full - jnp.mean(full, axis=-1, keepdims=True)
    variance = jnp.mean(centred * centred, axis=-1, keepdims=True)
    normed = (centred * lax.rsqrt(variance + STABILIZER_TINY) * gain[...]).astype(bf16)
    qkv = jnp.dot(normed, weights[:, 2 * width : 5 * width], preferred_element_type=f32)
    qkv = qkv.astype(bf16)

    tokens_in = latents * cells
    quarter_labels = [place[2 + k] for k in range(4)]

    def labels_of(shape, axis):
        cell = lax.rem(lax.broadcasted_iota(jnp.int32, shape, axis), cells)
        label = jnp.full(shape, -1, jnp.int32)
        for k in range(3, -1, -1):
            label = jnp.where(cell < CELLS * (k + 1), quarter_labels[k], label)
        return label

    allowed = labels_of((tokens_in, tokens_in), 0) == labels_of((tokens_in, tokens_in), 1)
    head_dim = width // heads
    pair = 2 * head_dim
    lane = lax.broadcasted_iota(jnp.int32, (1, pair), 1)
    left = jnp.where(lane < head_dim, 1.0, 0.0)
    sides = (left.astype(bf16), (1.0 - left).astype(bf16))
    attended = []
    for h in range(heads // 2):
        q = qkv[:, h * pair : (h + 1) * pair]
        k = qkv[:, width + h * pair : width + (h + 1) * pair]
        v = qkv[:, 2 * width + h * pair : 2 * width + (h + 1) * pair]
        both = []
        for side in sides:
            logits = lax.dot_general(
                q * side, k, (((1,), (1,)), ((), ())), preferred_element_type=f32
            )
            logits = jnp.where(allowed, logits / head_dim**0.5, -1e30)
            grown = jnp.exp(logits - jnp.max(logits, axis=-1, keepdims=True))
            grown = grown / jnp.sum(grown, axis=-1, keepdims=True)
            both.append(jnp.dot(grown.astype(bf16), v, preferred_element_type=f32))
        attended.append(jnp.where(lane < head_dim, both[0], both[1]).astype(bf16))
    attended = jnp.concatenate(attended, axis=1)
    result = jnp.dot(attended, weights[:, 5 * width :], preferred_element_type=f32)
    result = (full + result.astype(bf16).astype(f32)).astype(bf16)
    out[...] = result.reshape(latents, cells, width)


def body(
    level_tokens,
    hidden_probe_match_matrix,
    value_weight,
    pool_out_weight,
    latent_base,
    norm_gain,
    qkv_weight,
    attn_out_weight,
    region_ids,
):
    levels, row_count, col_count, width = level_tokens.shape
    latents, pool_heads, _ = hidden_probe_match_matrix.shape
    lat_count, lon_count = lax.axis_size("lat"), lax.axis_size("lon")
    i, j = lax.axis_index("lat"), lax.axis_index("lon")
    odd = j % 2
    quad = (i // LAT_RING + 2 * (i % LAT_RING)) % LAT_RING

    joined = jnp.concatenate([value_weight, pool_out_weight, qkv_weight, attn_out_weight], axis=1)
    piece_rows, all_columns = joined.shape
    columns = all_columns // (2 * LAT_RING)
    both = lax.dynamic_slice(joined, (0, quad * 2 * columns), (piece_rows, 2 * columns))
    mine = jnp.stack([both[:, :columns], both[:, columns:]])
    mine = jnp.broadcast_to(mine[None], (lon_count // 2, 2, piece_rows, columns))
    mine = mine.reshape(lon_count, piece_rows, columns)
    mine = lax.all_to_all(mine, "lon", 0, 0, tiled=True)
    mine = mine.reshape(lon_count * piece_rows, columns)

    def quarter(rows_at, cols_at):
        part = lax.dynamic_slice(
            level_tokens, (0, rows_at, cols_at, 0), (levels, HALF_LAT, HALF_LON, width)
        )
        return part.reshape(levels, CELLS, width)

    kept, sent = HALF_LAT * (1 - odd), HALF_LAT * odd
    corners = region_ids[::HALF_LAT, ::HALF_LON].reshape(4)
    plane = jnp.repeat(corners.astype(jnp.bfloat16), 4).reshape(1, 16, 1)
    plane = jnp.pad(plane, ((0, 0), (0, CELLS - 16), (0, 0)))
    plane = jnp.broadcast_to(plane, (1, CELLS, width))
    from_band = fetch(jnp.concatenate([quarter(sent, HALF_LON), plane], axis=0), along)
    from_corner = fetch(quarter(kept, 0), across)
    from_east = fetch(quarter(sent, 0), beside)

    parts = [mine] + [fetch(mine, source) for _, source in SLICE_STEPS]
    own_slices = jnp.stack(parts)
    other_slices = fetch(own_slices, other_core)

    theirs = from_band[levels, 0:16:4, 0].astype(jnp.int32)
    corners = jnp.where(odd == 0, corners, theirs)
    window = jnp.where(odd == 0, i, (i + lat_count - 1) % lat_count)
    wraps = (window == lat_count - 1).astype(jnp.int32)
    north = corners[:2] * 2
    south = corners[2:] * 2 + wraps
    labels = jnp.where(
        odd == 0, jnp.concatenate([north, south]), jnp.concatenate([south, north])
    )
    place = jnp.concatenate([jnp.stack([quad, odd]).astype(jnp.int32), labels])
    empty = jnp.zeros((levels, PADDED - 4 * CELLS, width), level_tokens.dtype)
    tokens = jnp.concatenate(
        [quarter(kept, HALF_LON), from_east, from_band[:levels], from_corner, empty], axis=1
    )

    vmem = pl.BlockSpec(memory_space=pltpu.VMEM)
    token_rows = levels * PADDED
    out = pl.pallas_call(
        functools.partial(window_kernel, HEADS, pool_heads),
        out_shape=jax.ShapeDtypeStruct((latents, PADDED, width), jnp.bfloat16),
        in_specs=[pl.BlockSpec(memory_space=pltpu.SMEM)] + [vmem] * 6,
        out_specs=vmem,
        scratch_shapes=[
            pltpu.VMEM((width, all_columns), jnp.bfloat16),
            pltpu.VMEM((token_rows, width), jnp.float32),
        ],
        compiler_params=pltpu.CompilerParams(vmem_limit_bytes=36 * 1024 * 1024),
        name="window",
    )(
        place,
        tokens,
        hidden_probe_match_matrix.reshape(latents * pool_heads, width),
        own_slices,
        other_slices,
        latent_base,
        norm_gain.reshape(1, width),
    )

    def part_of(k):
        return out[:, k * CELLS : (k + 1) * CELLS].reshape(latents, HALF_LAT, HALF_LON, width)

    to_band = give_back(part_of(2), along)
    to_corner = give_back(part_of(3), across)
    to_east = give_back(part_of(1), beside)
    kept_rows = jnp.concatenate([to_corner, part_of(0)], axis=2)
    other_rows = jnp.concatenate([to_east, to_band], axis=2)
    return jnp.where(
        odd == 0,
        jnp.concatenate([other_rows, kept_rows], axis=1),
        jnp.concatenate([kept_rows, other_rows], axis=1),
    )


def solution(mesh):
    placed = (
        P(None, "lat", "lon", None),
        P(),
        P("lon", None),
        P("lon", None),
        P(),
        P(),
        P("lon", None),
        P("lon", None),
        P("lat", "lon"),
    )
    return jax.shard_map(
        body, mesh=mesh, in_specs=placed, out_specs=P(None, "lat", "lon", None), check_vma=False
    )
```

```python
import functools

import jax
import jax.numpy as jnp
from jax import lax
from jax.experimental import pallas as pl
from jax.experimental.pallas import tpu as pltpu
from jax.sharding import PartitionSpec as P

HEADS = 8
LATENTS = 3
WIN_LAT = 6
WIN_LON = 12
HALF_LAT = WIN_LAT // 2
HALF_LON = WIN_LON // 2
CELLS = HALF_LAT * HALF_LON
PADDED = 80
LAT_RING = 4
STABILIZER_TINY = 1e-05
BOTH = ("lat", "lon")
LIMIT = 24 * 1024 * 1024


def pairs(source_of, lat_count, lon_count):
    route = []
    for i in range(lat_count):
        for j in range(lon_count):
            si, sj = source_of(i, j)
            source = (si % lat_count) * lon_count + sj % lon_count
            route.append((source, i * lon_count + j))
    return route


def fetch(block, source_of):
    route = pairs(source_of, lax.axis_size("lat"), lax.axis_size("lon"))
    return lax.ppermute(block, BOTH, route)


def give_back(block, source_of):
    route = pairs(source_of, lax.axis_size("lat"), lax.axis_size("lon"))
    return lax.ppermute(block, BOTH, [(b, a) for a, b in route])


def band_of(j):
    return 1 if j % 2 == 0 else -1


def beside(i, j):
    return i, j + 1


def along(i, j):
    return i + band_of(j), j


def across(i, j):
    return i + band_of(j), j + 1


def next_along_x(i, j):
    return i + band_of(j) * LAT_RING, j


def other_core(i, j):
    return i, j + 1 if j % 2 == 0 else j - 1


def quarter_kernel(place, regions, far_tokens, own, east, band, corner, tokens, rows, arrived):
    levels = tokens.shape[0]
    copies = [
        pltpu.make_async_copy(far_tokens.at[level], tokens.at[level], arrived.at[level])
        for level in range(levels)
    ]
    for copy in copies:
        copy.start()
    odd = place[1]
    kept, sent = HALF_LAT * (1 - odd), HALF_LAT * odd
    for k in range(4):
        label = regions[HALF_LAT * (k // 2), HALF_LON * (k % 2)]
        label = jnp.full((1, rows.shape[1]), label, jnp.int32)
        rows[levels * CELLS + k : levels * CELLS + k + 1] = label.astype(jnp.float32)
    rows[levels * CELLS + 4 :] = jnp.zeros((2, rows.shape[1]), jnp.float32)
    for n, (out, top, left) in enumerate(
        ((band, sent, HALF_LON), (corner, kept, 0), (east, sent, 0), (own, kept, HALF_LON))
    ):
        for level in range(levels):
            if n == 0:
                copies[level].wait()
            for r in range(HALF_LAT):
                row = tokens[level, top + r].astype(jnp.float32)
                at = level * CELLS + r * HALF_LON
                rows[at : at + HALF_LON] = row[left : left + HALF_LON]
        out[...] = rows[...].astype(out.dtype)


def mix_kernel(levels, place, own, east, band, corner, probe, tokens, mix, labels, joined):
    width = own.shape[1]
    cells = PADDED
    for k, part in enumerate((own, east, band, corner)):
        rows = part[...].astype(jnp.float32)
        for level in range(levels):
            joined[level, k * CELLS : (k + 1) * CELLS] = rows[level * CELLS : (level + 1) * CELLS]
    joined[:, 4 * CELLS :] = jnp.zeros((levels, cells - 4 * CELLS, width), jnp.float32)
    x = joined[...].astype(jnp.bfloat16).reshape(levels * cells, width)
    tokens[...] = x
    scores = lax.dot_general(
        x, probe[...], (((1,), (1,)), ((), ())), preferred_element_type=jnp.float32
    )
    scores = scores.reshape(levels, cells, probe.shape[0])
    scores = jnp.exp(scores - jnp.max(scores, axis=0, keepdims=True))
    weights = scores / jnp.sum(scores, axis=0, keepdims=True)
    mix[...] = weights.astype(jnp.bfloat16).reshape(levels * cells, probe.shape[0])
    at = levels * CELLS
    near = own[...].astype(jnp.float32)[at : at + 4, :128]
    far = band[...].astype(jnp.float32)[at : at + 4, :128]
    odd = jnp.full((4, 128), place[1], jnp.int32)
    ids = 2.0 * jnp.where(odd == 0, near, far)
    north = ids[:2]
    south = ids[2:] + jnp.full((2, 128), place[2], jnp.int32).astype(jnp.float32)
    first = odd[:2] == 0
    labels[:2] = jnp.where(first, north, south)
    labels[2:4] = jnp.where(first, south, north)
    labels[4:] = jnp.zeros((4, 128), jnp.float32)


def window_kernel(
    heads,
    pool_heads,
    place,
    tokens,
    mix,
    mine,
    ahead,
    mine_swapped,
    ahead_swapped,
    labels,
    base,
    gain,
    out,
    weights,
    values,
):
    latents, width = base.shape
    cells = PADDED
    level_count = tokens.shape[0] // cells
    columns = mine.shape[1]
    f32 = jnp.float32
    bf16 = jnp.bfloat16
    parity, core = place[0], place[1]
    for ref, group, side in (
        (mine, parity, core),
        (ahead, 1 - parity, core),
        (mine_swapped, parity, 1 - core),
        (ahead_swapped, 1 - parity, 1 - core),
    ):
        start = (group * 2 + side) * columns
        weights[:, pl.ds(pl.multiple_of(start, 128), columns)] = ref[...]

    values[...] = jnp.dot(tokens[...], weights[:, :width], preferred_element_type=f32)
    span = width // pool_heads
    head_of = lax.broadcasted_iota(jnp.int32, (latents * pool_heads, width), 1) // span
    row_of = lax.broadcasted_iota(jnp.int32, (latents * pool_heads, width), 0)
    pooled = []
    for m in range(latents):
        spread = jnp.where(row_of == head_of + m * pool_heads, 1.0, 0.0).astype(bf16)
        share = jnp.dot(mix[...], spread, preferred_element_type=f32) * values[...]
        pooled.append(jnp.sum(share.reshape(level_count, cells, width), axis=0).astype(bf16))
    pooled = jnp.concatenate(pooled, axis=0)
    latent = jnp.dot(pooled, weights[:, width : 2 * width], preferred_element_type=f32)
    base_rows = jnp.broadcast_to(base[...].astype(f32)[:, None, :], (latents, cells, width))
    latent = (latent + base_rows.reshape(latents * cells, width)).astype(bf16)

    full = latent.astype(f32)
    centred = full - jnp.mean(full, axis=-1, keepdims=True)
    variance = jnp.mean(centred * centred, axis=-1, keepdims=True)
    normed = (centred * lax.rsqrt(variance + STABILIZER_TINY) * gain[...]).astype(bf16)
    qkv = jnp.dot(normed, weights[:, 2 * width : 5 * width], preferred_element_type=f32)
    qkv = qkv.astype(bf16)

    tokens_in = latents * cells
    quarter_labels = [labels[k : k + 1, 0:1] for k in range(4)]

    def labels_of(shape, axis):
        cell = lax.rem(lax.broadcasted_iota(jnp.int32, shape, axis), cells)
        label = jnp.full(shape, -1.0, jnp.float32)
        for k in range(3, -1, -1):
            label = jnp.where(
                cell < CELLS * (k + 1), jnp.broadcast_to(quarter_labels[k], shape), label
            )
        return label

    allowed = labels_of((tokens_in, 1), 0) == labels_of((1, tokens_in), 1)
    head_dim = width // heads
    pair = 2 * head_dim
    lane = lax.broadcasted_iota(jnp.int32, (1, pair), 1)
    left = jnp.where(lane < head_dim, 1.0, 0.0)
    sides = (left.astype(bf16), (1.0 - left).astype(bf16))
    attended = []
    for h in range(heads // 2):
        q = qkv[:, h * pair : (h + 1) * pair]
        k = qkv[:, width + h * pair : width + (h + 1) * pair]
        v = qkv[:, 2 * width + h * pair : 2 * width + (h + 1) * pair]
        both = []
        for side in sides:
            logits = lax.dot_general(
                q * side, k, (((1,), (1,)), ((), ())), preferred_element_type=f32
            )
            logits = jnp.where(allowed, logits / head_dim**0.5, -1e30)
            grown = jnp.exp(logits - jnp.max(logits, axis=-1, keepdims=True))
            grown = grown / jnp.sum(grown, axis=-1, keepdims=True)
            both.append(jnp.dot(grown.astype(bf16), v, preferred_element_type=f32))
        attended.append(jnp.where(lane < head_dim, both[0], both[1]).astype(bf16))
    attended = jnp.concatenate(attended, axis=1)
    result = jnp.dot(attended, weights[:, 5 * width :], preferred_element_type=f32)
    result = (full + result.astype(bf16).astype(f32)).astype(bf16)
    out[...] = result.reshape(latents, cells, width)


def body(
    level_tokens,
    hidden_probe_match_matrix,
    value_weight,
    pool_out_weight,
    latent_base,
    norm_gain,
    qkv_weight,
    attn_out_weight,
    region_ids,
):
    levels, row_count, col_count, width = level_tokens.shape
    latents, pool_heads, _ = hidden_probe_match_matrix.shape
    lat_count, lon_count = lax.axis_size("lat"), lax.axis_size("lon")
    i, j = lax.axis_index("lat"), lax.axis_index("lon")
    odd = j % 2
    parity = (i // LAT_RING) % 2

    joined = jnp.concatenate([value_weight, pool_out_weight, qkv_weight, attn_out_weight], axis=1)
    piece_rows, all_columns = joined.shape
    columns = all_columns // 4
    both = lax.dynamic_slice(joined, (0, parity * 2 * columns), (piece_rows, 2 * columns))
    mine = jnp.stack([both[:, :columns], both[:, columns:]])
    mine = jnp.broadcast_to(mine[None], (lon_count // 2, 2, piece_rows, columns))
    mine = mine.reshape(lon_count, piece_rows, columns)
    mine = lax.all_to_all(mine, "lon", 0, 0, tiled=True)
    mine = mine.reshape(lon_count * piece_rows, columns)

    vmem = pl.BlockSpec(memory_space=pltpu.VMEM)
    smem = pl.BlockSpec(memory_space=pltpu.SMEM)
    window = jnp.where(odd == 0, i, (i + lat_count - 1) % lat_count)
    place = jnp.stack([parity, odd, (window == lat_count - 1).astype(jnp.int32)]).astype(jnp.int32)
    packed = levels * CELLS + 6
    quarter = jax.ShapeDtypeStruct((packed, width), level_tokens.dtype)
    own, east, band, corner = pl.pallas_call(
        quarter_kernel,
        out_shape=[quarter] * 4,
        in_specs=[smem, smem, pl.BlockSpec(memory_space=pl.ANY)],
        out_specs=[vmem] * 4,
        scratch_shapes=[
            pltpu.VMEM(level_tokens.shape, level_tokens.dtype),
            pltpu.VMEM((packed, width), jnp.float32),
            pltpu.SemaphoreType.DMA((levels,)),
        ],
        compiler_params=pltpu.CompilerParams(vmem_limit_bytes=LIMIT),
        name="quarters",
    )(place, region_ids, level_tokens)
    band = fetch(band, along)
    corner = fetch(corner, across)
    mine, band, corner, east = lax.optimization_barrier((mine, band, corner, east))
    ahead = fetch(mine, next_along_x)
    east = fetch(east, beside)

    again, east = lax.optimization_barrier((mine, east))
    mine_swapped = fetch(again, other_core)
    ahead, east = lax.optimization_barrier((ahead, east))
    token_rows = levels * PADDED
    mixes = latents * pool_heads
    tokens, mix, labels = pl.pallas_call(
        functools.partial(mix_kernel, levels),
        out_shape=[
            jax.ShapeDtypeStruct((token_rows, width), jnp.bfloat16),
            jax.ShapeDtypeStruct((token_rows, mixes), jnp.bfloat16),
            jax.ShapeDtypeStruct((8, 128), jnp.float32),
        ],
        in_specs=[smem] + [vmem] * 5,
        out_specs=[vmem] * 3,
        scratch_shapes=[pltpu.VMEM((levels, PADDED, width), jnp.float32)],
        compiler_params=pltpu.CompilerParams(vmem_limit_bytes=LIMIT),
        cost_estimate=pl.CostEstimate(
            flops=2 * token_rows * width * mixes, bytes_accessed=8 << 20, transcendentals=0
        ),
        name="mix",
    )(place, own, east, band, corner, hidden_probe_match_matrix.reshape(mixes, width))

    ahead_swapped = fetch(ahead, other_core)
    out = pl.pallas_call(
        functools.partial(window_kernel, HEADS, pool_heads),
        out_shape=jax.ShapeDtypeStruct((latents, PADDED, width), jnp.bfloat16),
        in_specs=[smem] + [vmem] * 9,
        out_specs=vmem,
        scratch_shapes=[
            pltpu.VMEM((width, all_columns), jnp.bfloat16),
            pltpu.VMEM((token_rows, width), jnp.float32),
        ],
        compiler_params=pltpu.CompilerParams(vmem_limit_bytes=LIMIT),
        name="window",
    )(
        place,
        tokens,
        mix,
        mine,
        ahead,
        mine_swapped,
        ahead_swapped,
        labels,
        latent_base,
        norm_gain.reshape(1, width),
    )

    def part_of(k):
        return out[:, k * CELLS : (k + 1) * CELLS].reshape(latents, HALF_LAT, HALF_LON, width)

    to_band = give_back(part_of(2), along)
    to_corner = give_back(part_of(3), across)
    to_east = give_back(part_of(1), beside)
    kept_rows = jnp.concatenate([to_corner, part_of(0)], axis=2)
    other_rows = jnp.concatenate([to_east, to_band], axis=2)
    return jnp.where(
        odd == 0,
        jnp.concatenate([other_rows, kept_rows], axis=1),
        jnp.concatenate([kept_rows, other_rows], axis=1),
    )


def solution(mesh):
    placed = (
        P(None, "lat", "lon", None),
        P(),
        P("lon", None),
        P("lon", None),
        P(),
        P(),
        P("lon", None),
        P("lon", None),
        P("lat", "lon"),
    )
    return jax.shard_map(
        body, mesh=mesh, in_specs=placed, out_specs=P(None, "lat", "lon", None), check_vma=False
    )
```

```python
import functools

import jax
import jax.numpy as jnp
from jax import lax
from jax.experimental import pallas as pl
from jax.experimental.pallas import tpu as pltpu
from jax.sharding import PartitionSpec as P

HEADS = 8
LATENTS = 3
WIN_LAT = 6
WIN_LON = 12
HALF_LAT = WIN_LAT // 2
HALF_LON = WIN_LON // 2
CELLS = HALF_LAT * HALF_LON
PADDED = 80
LAT_RING = 4
STABILIZER_TINY = 1e-05
BOTH = ("lat", "lon")
LIMIT = 24 * 1024 * 1024


def pairs(source_of, lat_count, lon_count):
    route = []
    for i in range(lat_count):
        for j in range(lon_count):
            si, sj = source_of(i, j)
            source = (si % lat_count) * lon_count + sj % lon_count
            route.append((source, i * lon_count + j))
    return route


def fetch(block, source_of):
    route = pairs(source_of, lax.axis_size("lat"), lax.axis_size("lon"))
    return lax.ppermute(block, BOTH, route)


def give_back(block, source_of):
    route = pairs(source_of, lax.axis_size("lat"), lax.axis_size("lon"))
    return lax.ppermute(block, BOTH, [(b, a) for a, b in route])


def band_of(j):
    return 1 if j % 2 == 0 else -1


def beside(i, j):
    return i, j + 1


def along(i, j):
    return i + band_of(j), j


def across(i, j):
    return i + band_of(j), j + 1


def next_along_x(i, j):
    return i + band_of(j) * LAT_RING, j


def other_core(i, j):
    return i, j + 1 if j % 2 == 0 else j - 1


def quarter_kernel(place, regions, tokens, own, east, band, corner, rows):
    levels = tokens.shape[2]
    odd = place[1]
    kept, sent = HALF_LAT * (1 - odd), HALF_LAT * odd
    for k in range(4):
        label = regions[HALF_LAT * (k // 2), HALF_LON * (k % 2)]
        label = jnp.full((1, rows.shape[1]), label, jnp.int32)
        rows[levels * CELLS + k : levels * CELLS + k + 1] = label.astype(jnp.float32)
    rows[levels * CELLS + 4 :] = jnp.zeros((2, rows.shape[1]), jnp.float32)
    for out, top, left in (
        (band, sent, HALF_LON),
        (corner, kept, 0),
        (east, sent, 0),
        (own, kept, HALF_LON),
    ):
        for r in range(HALF_LAT):
            for c in range(HALF_LON):
                at = (r * HALF_LON + c) * levels
                rows[at : at + levels] = tokens[top + r, left + c].astype(jnp.float32)
        out[...] = rows[...].astype(out.dtype)


def mix_kernel(levels, place, own, east, band, corner, probe, tokens, mix, labels, rows, joined):
    width = own.shape[1]
    cells = PADDED
    for k, part in enumerate((own, east, band, corner)):
        for t in range(rows.shape[0]):
            rows[t] = part[:, t * 128 : (t + 1) * 128].astype(jnp.float32)
            for level in range(levels):
                at = pl.ds(level, CELLS, stride=levels)
                joined[level, k * CELLS : (k + 1) * CELLS, t * 128 : (t + 1) * 128] = rows[t, at]
    joined[:, 4 * CELLS :] = jnp.zeros((levels, cells - 4 * CELLS, width), jnp.float32)
    x = joined[...].astype(jnp.bfloat16).reshape(levels * cells, width)
    tokens[...] = x
    scores = lax.dot_general(
        x, probe[...], (((1,), (1,)), ((), ())), preferred_element_type=jnp.float32
    )
    scores = scores.reshape(levels, cells, probe.shape[0])
    scores = jnp.exp(scores - jnp.max(scores, axis=0, keepdims=True))
    weights = scores / jnp.sum(scores, axis=0, keepdims=True)
    mix[...] = weights.astype(jnp.bfloat16).reshape(levels * cells, probe.shape[0])
    at = levels * CELLS
    near = own[...].astype(jnp.float32)[at : at + 4, :128]
    far = band[...].astype(jnp.float32)[at : at + 4, :128]
    odd = jnp.full((4, 128), place[1], jnp.int32)
    ids = 2.0 * jnp.where(odd == 0, near, far)
    north = ids[:2]
    south = ids[2:] + jnp.full((2, 128), place[2], jnp.int32).astype(jnp.float32)
    first = odd[:2] == 0
    labels[:2] = jnp.where(first, north, south)
    labels[2:4] = jnp.where(first, south, north)
    labels[4:] = jnp.zeros((4, 128), jnp.float32)


def window_kernel(
    heads,
    pool_heads,
    place,
    tokens,
    mix,
    mine,
    ahead,
    mine_swapped,
    ahead_swapped,
    labels,
    base,
    gain,
    out,
    weights,
    values,
):
    latents, width = base.shape
    cells = PADDED
    level_count = tokens.shape[0] // cells
    columns = mine.shape[1]
    f32 = jnp.float32
    bf16 = jnp.bfloat16
    parity, core = place[0], place[1]
    for ref, group, side in (
        (mine, parity, core),
        (ahead, 1 - parity, core),
        (mine_swapped, parity, 1 - core),
        (ahead_swapped, 1 - parity, 1 - core),
    ):
        start = (group * 2 + side) * columns
        weights[:, pl.ds(pl.multiple_of(start, 128), columns)] = ref[...]

    values[...] = jnp.dot(tokens[...], weights[:, :width], preferred_element_type=f32)
    span = width // pool_heads
    head_of = lax.broadcasted_iota(jnp.int32, (latents * pool_heads, width), 1) // span
    row_of = lax.broadcasted_iota(jnp.int32, (latents * pool_heads, width), 0)
    pooled = []
    for m in range(latents):
        spread = jnp.where(row_of == head_of + m * pool_heads, 1.0, 0.0).astype(bf16)
        share = jnp.dot(mix[...], spread, preferred_element_type=f32) * values[...]
        pooled.append(jnp.sum(share.reshape(level_count, cells, width), axis=0).astype(bf16))
    pooled = jnp.concatenate(pooled, axis=0)
    latent = jnp.dot(pooled, weights[:, width : 2 * width], preferred_element_type=f32)
    base_rows = jnp.broadcast_to(base[...].astype(f32)[:, None, :], (latents, cells, width))
    latent = (latent + base_rows.reshape(latents * cells, width)).astype(bf16)

    full = latent.astype(f32)
    centred = full - jnp.mean(full, axis=-1, keepdims=True)
    variance = jnp.mean(centred * centred, axis=-1, keepdims=True)
    normed = (centred * lax.rsqrt(variance + STABILIZER_TINY) * gain[...]).astype(bf16)
    qkv = jnp.dot(normed, weights[:, 2 * width : 5 * width], preferred_element_type=f32)
    qkv = qkv.astype(bf16)

    tokens_in = latents * cells
    quarter_labels = [labels[k : k + 1, 0:1] for k in range(4)]

    def labels_of(shape, axis):
        cell = lax.rem(lax.broadcasted_iota(jnp.int32, shape, axis), cells)
        label = jnp.full(shape, -1.0, jnp.float32)
        for k in range(3, -1, -1):
            label = jnp.where(
                cell < CELLS * (k + 1), jnp.broadcast_to(quarter_labels[k], shape), label
            )
        return label

    allowed = labels_of((tokens_in, 1), 0) == labels_of((1, tokens_in), 1)
    head_dim = width // heads
    pair = 2 * head_dim
    lane = lax.broadcasted_iota(jnp.int32, (1, pair), 1)
    left = jnp.where(lane < head_dim, 1.0, 0.0)
    scale = head_dim**-0.5
    sides = ((left * scale).astype(bf16), ((1.0 - left) * scale).astype(bf16))
    ones = jnp.ones((tokens_in, pair), bf16)
    attended = []
    for h in range(heads // 2):
        q = qkv[:, h * pair : (h + 1) * pair]
        k = qkv[:, width + h * pair : width + (h + 1) * pair]
        v = qkv[:, 2 * width + h * pair : 2 * width + (h + 1) * pair]
        v = jnp.concatenate([v, ones], axis=1)
        both = []
        for side in sides:
            logits = lax.dot_general(
                q * side, k, (((1,), (1,)), ((), ())), preferred_element_type=f32
            )
            logits = jnp.where(allowed, logits, -1e30)
            grown = jnp.exp(logits - jnp.max(logits, axis=-1, keepdims=True)).astype(bf16)
            both.append(jnp.dot(grown, v, preferred_element_type=f32))
        total = jnp.where(lane < head_dim, both[0][:, pair:], both[1][:, pair:])
        sums = jnp.where(lane < head_dim, both[0][:, :pair], both[1][:, :pair])
        attended.append((sums / total).astype(bf16))
    attended = jnp.concatenate(attended, axis=1)
    result = jnp.dot(attended, weights[:, 5 * width :], preferred_element_type=f32)
    result = (full + result.astype(bf16).astype(f32)).astype(bf16)
    out[...] = result.reshape(latents, cells, width)


def body(
    level_tokens,
    hidden_probe_match_matrix,
    value_weight,
    pool_out_weight,
    latent_base,
    norm_gain,
    qkv_weight,
    attn_out_weight,
    region_ids,
):
    levels, row_count, col_count, width = level_tokens.shape
    latents, pool_heads, _ = hidden_probe_match_matrix.shape
    lat_count, lon_count = lax.axis_size("lat"), lax.axis_size("lon")
    i, j = lax.axis_index("lat"), lax.axis_index("lon")
    odd = j % 2
    parity = (i // LAT_RING) % 2

    joined = jnp.concatenate([value_weight, pool_out_weight, qkv_weight, attn_out_weight], axis=1)
    piece_rows, all_columns = joined.shape
    columns = all_columns // 4
    both = lax.dynamic_slice(joined, (0, parity * 2 * columns), (piece_rows, 2 * columns))
    mine = jnp.stack([both[:, :columns], both[:, columns:]])
    mine = jnp.broadcast_to(mine[None], (lon_count // 2, 2, piece_rows, columns))
    mine = mine.reshape(lon_count, piece_rows, columns)
    mine = lax.all_to_all(mine, "lon", 0, 0, tiled=True)
    mine = mine.reshape(lon_count * piece_rows, columns)

    vmem = pl.BlockSpec(memory_space=pltpu.VMEM)
    smem = pl.BlockSpec(memory_space=pltpu.SMEM)
    window = jnp.where(odd == 0, i, (i + lat_count - 1) % lat_count)
    place = jnp.stack([parity, odd, (window == lat_count - 1).astype(jnp.int32)]).astype(jnp.int32)
    packed = levels * CELLS + 6
    quarter = jax.ShapeDtypeStruct((packed, width), level_tokens.dtype)
    own, east, band, corner = pl.pallas_call(
        quarter_kernel,
        out_shape=[quarter] * 4,
        in_specs=[smem, smem, vmem],
        out_specs=[vmem] * 4,
        scratch_shapes=[pltpu.VMEM((packed, width), jnp.float32)],
        compiler_params=pltpu.CompilerParams(vmem_limit_bytes=LIMIT),
        name="quarters",
    )(place, region_ids, jnp.transpose(level_tokens, (1, 2, 0, 3)))
    band = fetch(band, along)
    corner = fetch(corner, across)
    mine, band, corner, east = lax.optimization_barrier((mine, band, corner, east))
    ahead = fetch(mine, next_along_x)
    east = fetch(east, beside)

    mine_swapped = fetch(mine, other_core)
    ahead, east = lax.optimization_barrier((ahead, east))
    token_rows = levels * PADDED
    mixes = latents * pool_heads
    tokens, mix, labels = pl.pallas_call(
        functools.partial(mix_kernel, levels),
        out_shape=[
            jax.ShapeDtypeStruct((token_rows, width), jnp.bfloat16),
            jax.ShapeDtypeStruct((token_rows, mixes), jnp.bfloat16),
            jax.ShapeDtypeStruct((8, 128), jnp.float32),
        ],
        in_specs=[smem] + [vmem] * 5,
        out_specs=[vmem] * 3,
        scratch_shapes=[
            pltpu.VMEM((width // 128, packed, 128), jnp.float32),
            pltpu.VMEM((levels, PADDED, width), jnp.float32),
        ],
        compiler_params=pltpu.CompilerParams(vmem_limit_bytes=LIMIT),
        cost_estimate=pl.CostEstimate(
            flops=2 * token_rows * width * mixes, bytes_accessed=8 << 20, transcendentals=0
        ),
        name="mix",
    )(place, own, east, band, corner, hidden_probe_match_matrix.reshape(mixes, width))

    ahead_swapped = fetch(ahead, other_core)
    out = pl.pallas_call(
        functools.partial(window_kernel, HEADS, pool_heads),
        out_shape=jax.ShapeDtypeStruct((latents, PADDED, width), jnp.bfloat16),
        in_specs=[smem] + [vmem] * 9,
        out_specs=vmem,
        scratch_shapes=[
            pltpu.VMEM((width, all_columns), jnp.bfloat16),
            pltpu.VMEM((token_rows, width), jnp.float32),
        ],
        compiler_params=pltpu.CompilerParams(vmem_limit_bytes=LIMIT),
        name="window",
    )(
        place,
        tokens,
        mix,
        mine,
        ahead,
        mine_swapped,
        ahead_swapped,
        labels,
        latent_base,
        norm_gain.reshape(1, width),
    )

    def part_of(k):
        return out[:, k * CELLS : (k + 1) * CELLS].reshape(latents, HALF_LAT, HALF_LON, width)

    to_band = give_back(part_of(2), along)
    to_corner = give_back(part_of(3), across)
    to_east = give_back(part_of(1), beside)
    kept_rows = jnp.concatenate([to_corner, part_of(0)], axis=2)
    other_rows = jnp.concatenate([to_east, to_band], axis=2)
    return jnp.where(
        odd == 0,
        jnp.concatenate([other_rows, kept_rows], axis=1),
        jnp.concatenate([kept_rows, other_rows], axis=1),
    )


def solution(mesh):
    placed = (
        P(None, "lat", "lon", None),
        P(),
        P("lon", None),
        P("lon", None),
        P(),
        P(),
        P("lon", None),
        P("lon", None),
        P("lat", "lon"),
    )
    return jax.shard_map(
        body, mesh=mesh, in_specs=placed, out_specs=P(None, "lat", "lon", None), check_vma=False
    )
```

```python
import functools

import jax
import jax.numpy as jnp
from jax import lax
from jax.experimental import pallas as pl
from jax.experimental.pallas import tpu as pltpu
from jax.sharding import PartitionSpec as P

HEADS = 8
LATENTS = 3
WIN_LAT = 6
WIN_LON = 12
HALF_LAT = WIN_LAT // 2
HALF_LON = WIN_LON // 2
CELLS = HALF_LAT * HALF_LON
PADDED = 80
LAT_RING = 4
STABILIZER_TINY = 1e-05
BOTH = ("lat", "lon")
LIMIT = 24 * 1024 * 1024


def pairs(source_of, lat_count, lon_count):
    route = []
    for i in range(lat_count):
        for j in range(lon_count):
            si, sj = source_of(i, j)
            source = (si % lat_count) * lon_count + sj % lon_count
            route.append((source, i * lon_count + j))
    return route


def fetch(block, source_of):
    route = pairs(source_of, lax.axis_size("lat"), lax.axis_size("lon"))
    return lax.ppermute(block, BOTH, route)


def give_back(block, source_of):
    route = pairs(source_of, lax.axis_size("lat"), lax.axis_size("lon"))
    return lax.ppermute(block, BOTH, [(b, a) for a, b in route])


def band_of(j):
    return 1 if j % 2 == 0 else -1


def beside(i, j):
    return i, j + 1


def along(i, j):
    return i + band_of(j), j


def across(i, j):
    return i + band_of(j), j + 1


def next_along_x(i, j):
    return i + band_of(j) * LAT_RING, j


def other_core(i, j):
    return i, j + 1 if j % 2 == 0 else j - 1


def quarter_kernel(place, regions, tokens, own, east, band, corner, rows):
    levels = tokens.shape[2]
    odd = place[1]
    kept, sent = HALF_LAT * (1 - odd), HALF_LAT * odd
    for k in range(4):
        label = regions[HALF_LAT * (k // 2), HALF_LON * (k % 2)]
        label = jnp.full((1, rows.shape[1]), label, jnp.int32)
        rows[levels * CELLS + k : levels * CELLS + k + 1] = label.astype(jnp.float32)
    rows[levels * CELLS + 4 :] = jnp.zeros((2, rows.shape[1]), jnp.float32)
    for out, top, left in (
        (band, sent, HALF_LON),
        (corner, kept, 0),
        (east, sent, 0),
        (own, kept, HALF_LON),
    ):
        for r in range(HALF_LAT):
            for c in range(HALF_LON):
                at = (r * HALF_LON + c) * levels
                rows[at : at + levels] = tokens[top + r, left + c].astype(jnp.float32)
        out[...] = rows[...].astype(out.dtype)


def mix_kernel(levels, place, own, east, band, corner, probe, tokens, mix, labels, rows, joined):
    width = own.shape[1]
    cells = PADDED
    for k, part in enumerate((own, east, band, corner)):
        for t in range(rows.shape[0]):
            rows[t] = part[:, t * 128 : (t + 1) * 128].astype(jnp.float32)
            for level in range(levels):
                at = pl.ds(level, CELLS, stride=levels)
                joined[level, k * CELLS : (k + 1) * CELLS, t * 128 : (t + 1) * 128] = rows[t, at]
    joined[:, 4 * CELLS :] = jnp.zeros((levels, cells - 4 * CELLS, width), jnp.float32)
    x = joined[...].astype(jnp.bfloat16).reshape(levels * cells, width)
    tokens[...] = x
    scores = lax.dot_general(
        x, probe[...], (((1,), (1,)), ((), ())), preferred_element_type=jnp.float32
    )
    scores = scores.reshape(levels, cells, probe.shape[0])
    scores = jnp.exp(scores - jnp.max(scores, axis=0, keepdims=True))
    weights = scores / jnp.sum(scores, axis=0, keepdims=True)
    mix[...] = weights.astype(jnp.bfloat16).reshape(levels * cells, probe.shape[0])
    at = levels * CELLS
    near = own[...].astype(jnp.float32)[at : at + 4, :128]
    far = band[...].astype(jnp.float32)[at : at + 4, :128]
    odd = jnp.full((4, 128), place[1], jnp.int32)
    ids = 2.0 * jnp.where(odd == 0, near, far)
    north = ids[:2]
    south = ids[2:] + jnp.full((2, 128), place[2], jnp.int32).astype(jnp.float32)
    first = odd[:2] == 0
    labels[:2] = jnp.where(first, north, south)
    labels[2:4] = jnp.where(first, south, north)
    labels[4:] = jnp.zeros((4, 128), jnp.float32)


def window_kernel(
    heads,
    pool_heads,
    place,
    tokens,
    mix,
    mine,
    ahead,
    mine_swapped,
    ahead_swapped,
    labels,
    base,
    gain,
    out,
    weights,
    values,
):
    latents, width = base.shape
    cells = PADDED
    level_count = tokens.shape[0] // cells
    columns = mine.shape[2]
    f32 = jnp.float32
    bf16 = jnp.bfloat16
    parity, core = place[0], place[1]
    for ref, group, side in (
        (mine, parity, core),
        (ahead, 1 - parity, core),
        (mine_swapped, parity, 1 - core),
        (ahead_swapped, 1 - parity, 1 - core),
    ):
        start = pl.ds(pl.multiple_of(group * columns, 128), columns)
        weights[:, side, :, start] = ref[...]

    def weight(first, last):
        return weights[:, :, :, first:last].reshape(width, last - first)

    values[...] = jnp.dot(tokens[...], weight(0, width), preferred_element_type=f32)
    span = width // pool_heads
    head_of = lax.broadcasted_iota(jnp.int32, (latents * pool_heads, width), 1) // span
    row_of = lax.broadcasted_iota(jnp.int32, (latents * pool_heads, width), 0)
    pooled = []
    for m in range(latents):
        spread = jnp.where(row_of == head_of + m * pool_heads, 1.0, 0.0).astype(bf16)
        share = jnp.dot(mix[...], spread, preferred_element_type=f32) * values[...]
        pooled.append(jnp.sum(share.reshape(level_count, cells, width), axis=0).astype(bf16))
    pooled = jnp.concatenate(pooled, axis=0)
    latent = jnp.dot(pooled, weight(width, 2 * width), preferred_element_type=f32)
    base_rows = jnp.broadcast_to(base[...].astype(f32)[:, None, :], (latents, cells, width))
    latent = (latent + base_rows.reshape(latents * cells, width)).astype(bf16)

    full = latent.astype(f32)
    centred = full - jnp.mean(full, axis=-1, keepdims=True)
    variance = jnp.mean(centred * centred, axis=-1, keepdims=True)
    normed = (centred * lax.rsqrt(variance + STABILIZER_TINY) * gain[...]).astype(bf16)
    qkv = jnp.dot(normed, weight(2 * width, 5 * width), preferred_element_type=f32)
    qkv = qkv.astype(bf16)

    tokens_in = latents * cells
    quarter_labels = [labels[k : k + 1, 0:1] for k in range(4)]

    def labels_of(shape, axis):
        cell = lax.rem(lax.broadcasted_iota(jnp.int32, shape, axis), cells)
        label = jnp.full(shape, -1.0, jnp.float32)
        for k in range(3, -1, -1):
            label = jnp.where(
                cell < CELLS * (k + 1), jnp.broadcast_to(quarter_labels[k], shape), label
            )
        return label

    allowed = labels_of((tokens_in, 1), 0) == labels_of((1, tokens_in), 1)
    head_dim = width // heads
    pair = 2 * head_dim
    lane = lax.broadcasted_iota(jnp.int32, (1, pair), 1)
    left = jnp.where(lane < head_dim, 1.0, 0.0)
    scale = head_dim**-0.5
    sides = ((left * scale).astype(bf16), ((1.0 - left) * scale).astype(bf16))
    ones = jnp.ones((tokens_in, pair), bf16)
    attended = []
    for h in range(heads // 2):
        q = qkv[:, h * pair : (h + 1) * pair]
        k = qkv[:, width + h * pair : width + (h + 1) * pair]
        v = qkv[:, 2 * width + h * pair : 2 * width + (h + 1) * pair]
        v = jnp.concatenate([v, ones], axis=1)
        both = []
        for side in sides:
            logits = lax.dot_general(
                q * side, k, (((1,), (1,)), ((), ())), preferred_element_type=f32
            )
            logits = jnp.where(allowed, logits, -1e30)
            grown = jnp.exp(logits - jnp.max(logits, axis=-1, keepdims=True)).astype(bf16)
            both.append(jnp.dot(grown, v, preferred_element_type=f32))
        total = jnp.where(lane < head_dim, both[0][:, pair:], both[1][:, pair:])
        sums = jnp.where(lane < head_dim, both[0][:, :pair], both[1][:, :pair])
        attended.append((sums / total).astype(bf16))
    attended = jnp.concatenate(attended, axis=1)
    result = jnp.dot(attended, weight(5 * width, 6 * width), preferred_element_type=f32)
    result = (full + result.astype(bf16).astype(f32)).astype(bf16)
    out[...] = result.reshape(latents, cells, width)


def body(
    level_tokens,
    hidden_probe_match_matrix,
    value_weight,
    pool_out_weight,
    latent_base,
    norm_gain,
    qkv_weight,
    attn_out_weight,
    region_ids,
):
    levels, row_count, col_count, width = level_tokens.shape
    latents, pool_heads, _ = hidden_probe_match_matrix.shape
    lat_count, lon_count = lax.axis_size("lat"), lax.axis_size("lon")
    i, j = lax.axis_index("lat"), lax.axis_index("lon")
    odd = j % 2
    parity = (i // LAT_RING) % 2

    joined = jnp.concatenate([value_weight, pool_out_weight, qkv_weight, attn_out_weight], axis=1)
    piece_rows, all_columns = joined.shape
    half = all_columns // 2
    groups = lon_count // 2
    mine = lax.dynamic_slice(joined, (0, parity * half), (piece_rows, half))
    mine = jnp.broadcast_to(mine[None], (groups, piece_rows, half))
    same_core = [list(range(core, lon_count, 2)) for core in range(2)]
    mine = lax.all_to_all(mine, "lon", 0, 0, tiled=True, axis_index_groups=same_core)

    vmem = pl.BlockSpec(memory_space=pltpu.VMEM)
    smem = pl.BlockSpec(memory_space=pltpu.SMEM)
    window = jnp.where(odd == 0, i, (i + lat_count - 1) % lat_count)
    place = jnp.stack([parity, odd, (window == lat_count - 1).astype(jnp.int32)]).astype(jnp.int32)
    packed = levels * CELLS + 6
    quarter = jax.ShapeDtypeStruct((packed, width), level_tokens.dtype)
    own, east, band, corner = pl.pallas_call(
        quarter_kernel,
        out_shape=[quarter] * 4,
        in_specs=[smem, smem, vmem],
        out_specs=[vmem] * 4,
        scratch_shapes=[pltpu.VMEM((packed, width), jnp.float32)],
        compiler_params=pltpu.CompilerParams(vmem_limit_bytes=LIMIT),
        name="quarters",
    )(place, region_ids, jnp.transpose(level_tokens, (1, 2, 0, 3)))
    band = fetch(band, along)
    corner = fetch(corner, across)
    mine, band, corner, east = lax.optimization_barrier((mine, band, corner, east))
    ahead = fetch(mine, next_along_x)
    east = fetch(east, beside)

    mine_swapped = fetch(mine, other_core)
    ahead, east = lax.optimization_barrier((ahead, east))
    token_rows = levels * PADDED
    mixes = latents * pool_heads
    tokens, mix, labels = pl.pallas_call(
        functools.partial(mix_kernel, levels),
        out_shape=[
            jax.ShapeDtypeStruct((token_rows, width), jnp.bfloat16),
            jax.ShapeDtypeStruct((token_rows, mixes), jnp.bfloat16),
            jax.ShapeDtypeStruct((8, 128), jnp.float32),
        ],
        in_specs=[smem] + [vmem] * 5,
        out_specs=[vmem] * 3,
        scratch_shapes=[
            pltpu.VMEM((width // 128, packed, 128), jnp.float32),
            pltpu.VMEM((levels, PADDED, width), jnp.float32),
        ],
        compiler_params=pltpu.CompilerParams(vmem_limit_bytes=LIMIT),
        cost_estimate=pl.CostEstimate(
            flops=2 * token_rows * width * mixes, bytes_accessed=8 << 20, transcendentals=0
        ),
        name="mix",
    )(place, own, east, band, corner, hidden_probe_match_matrix.reshape(mixes, width))

    ahead_swapped = fetch(ahead, other_core)
    out = pl.pallas_call(
        functools.partial(window_kernel, HEADS, pool_heads),
        out_shape=jax.ShapeDtypeStruct((latents, PADDED, width), jnp.bfloat16),
        in_specs=[smem] + [vmem] * 9,
        out_specs=vmem,
        scratch_shapes=[
            pltpu.VMEM((groups, 2, piece_rows, all_columns), jnp.bfloat16),
            pltpu.VMEM((token_rows, width), jnp.float32),
        ],
        compiler_params=pltpu.CompilerParams(vmem_limit_bytes=LIMIT),
        name="window",
    )(
        place,
        tokens,
        mix,
        mine,
        ahead,
        mine_swapped,
        ahead_swapped,
        labels,
        latent_base,
        norm_gain.reshape(1, width),
    )

    def part_of(k):
        return out[:, k * CELLS : (k + 1) * CELLS].reshape(latents, HALF_LAT, HALF_LON, width)

    to_band = give_back(part_of(2), along)
    to_corner = give_back(part_of(3), across)
    to_east = give_back(part_of(1), beside)
    kept_rows = jnp.concatenate([to_corner, part_of(0)], axis=2)
    other_rows = jnp.concatenate([to_east, to_band], axis=2)
    return jnp.where(
        odd == 0,
        jnp.concatenate([other_rows, kept_rows], axis=1),
        jnp.concatenate([kept_rows, other_rows], axis=1),
    )


def solution(mesh):
    placed = (
        P(None, "lat", "lon", None),
        P(),
        P("lon", None),
        P("lon", None),
        P(),
        P(),
        P("lon", None),
        P("lon", None),
        P("lat", "lon"),
    )
    return jax.shard_map(
        body, mesh=mesh, in_specs=placed, out_specs=P(None, "lat", "lon", None), check_vma=False
    )
```

```python
import functools

import jax
import jax.numpy as jnp
from jax import lax
from jax.experimental import pallas as pl
from jax.experimental.pallas import tpu as pltpu
from jax.sharding import PartitionSpec as P

HEADS = 8
LATENTS = 3
WIN_LAT = 6
WIN_LON = 12
HALF_LAT = WIN_LAT // 2
HALF_LON = WIN_LON // 2
CELLS = HALF_LAT * HALF_LON
PADDED = 80
LAT_RING = 4
STABILIZER_TINY = 1e-05
BOTH = ("lat", "lon")
LIMIT = 24 * 1024 * 1024


def pairs(source_of, lat_count, lon_count):
    route = []
    for i in range(lat_count):
        for j in range(lon_count):
            si, sj = source_of(i, j)
            source = (si % lat_count) * lon_count + sj % lon_count
            route.append((source, i * lon_count + j))
    return route


def fetch(block, source_of):
    route = pairs(source_of, lax.axis_size("lat"), lax.axis_size("lon"))
    return lax.ppermute(block, BOTH, route)


def give_back(block, source_of):
    route = pairs(source_of, lax.axis_size("lat"), lax.axis_size("lon"))
    return lax.ppermute(block, BOTH, [(b, a) for a, b in route])


def band_of(j):
    return 1 if j % 2 == 0 else -1


def beside(i, j):
    return i, j + 1


def along(i, j):
    return i + band_of(j), j


def across(i, j):
    return i + band_of(j), j + 1


def next_along_x(i, j):
    return i + band_of(j) * LAT_RING, j


def other_core(i, j):
    return i, j + 1 if j % 2 == 0 else j - 1


def quarter_kernel(place, regions, tokens, own, east, band, corner, rows):
    levels = tokens.shape[2]
    odd = place[1]
    kept, sent = HALF_LAT * (1 - odd), HALF_LAT * odd
    for k in range(4):
        label = regions[HALF_LAT * (k // 2), HALF_LON * (k % 2)]
        label = jnp.full((1, rows.shape[1]), label, jnp.int32)
        rows[levels * CELLS + k : levels * CELLS + k + 1] = label.astype(jnp.float32)
    rows[levels * CELLS + 4 :] = jnp.zeros((2, rows.shape[1]), jnp.float32)
    for out, top, left in (
        (band, sent, HALF_LON),
        (corner, kept, 0),
        (east, sent, 0),
        (own, kept, HALF_LON),
    ):
        for r in range(HALF_LAT):
            for c in range(HALF_LON):
                at = (r * HALF_LON + c) * levels
                rows[at : at + levels] = tokens[top + r, left + c].astype(jnp.float32)
        out[...] = rows[...].astype(out.dtype)


def mix_kernel(levels, place, own, east, band, corner, probe, tokens, mix, labels, rows, joined):
    width = own.shape[1]
    cells = PADDED
    for k, part in enumerate((own, east, band, corner)):
        for t in range(rows.shape[0]):
            rows[t] = part[:, t * 128 : (t + 1) * 128].astype(jnp.float32)
            for level in range(levels):
                at = pl.ds(level, CELLS, stride=levels)
                joined[level, k * CELLS : (k + 1) * CELLS, t * 128 : (t + 1) * 128] = rows[t, at]
    joined[:, 4 * CELLS :] = jnp.zeros((levels, cells - 4 * CELLS, width), jnp.float32)
    x = joined[...].astype(jnp.bfloat16).reshape(levels * cells, width)
    tokens[...] = x
    scores = lax.dot_general(
        x, probe[...], (((1,), (1,)), ((), ())), preferred_element_type=jnp.float32
    )
    scores = scores.reshape(levels, cells, probe.shape[0])
    scores = jnp.exp(scores - jnp.max(scores, axis=0, keepdims=True))
    weights = scores / jnp.sum(scores, axis=0, keepdims=True)
    mix[...] = weights.astype(jnp.bfloat16).reshape(levels * cells, probe.shape[0])
    at = levels * CELLS
    near = own[...].astype(jnp.float32)[at : at + 4, :128]
    far = band[...].astype(jnp.float32)[at : at + 4, :128]
    odd = jnp.full((4, 128), place[1], jnp.int32)
    ids = 2.0 * jnp.where(odd == 0, near, far)
    north = ids[:2]
    south = ids[2:] + jnp.full((2, 128), place[2], jnp.int32).astype(jnp.float32)
    first = odd[:2] == 0
    labels[:2] = jnp.where(first, north, south)
    labels[2:4] = jnp.where(first, south, north)
    labels[4:] = jnp.zeros((4, 128), jnp.float32)


def window_kernel(
    heads,
    pool_heads,
    place,
    tokens,
    mix,
    mine,
    ahead,
    mine_swapped,
    ahead_swapped,
    labels,
    base,
    gain,
    own,
    east,
    band,
    corner,
    weights,
    values,
):
    latents, width = base.shape
    cells = PADDED
    level_count = tokens.shape[0] // cells
    columns = mine.shape[2]
    f32 = jnp.float32
    bf16 = jnp.bfloat16
    parity, core = place[0], place[1]
    for ref, group, side in (
        (mine, parity, core),
        (ahead, 1 - parity, core),
        (mine_swapped, parity, 1 - core),
        (ahead_swapped, 1 - parity, 1 - core),
    ):
        start = pl.ds(pl.multiple_of(group * columns, 128), columns)
        weights[:, side, :, start] = ref[...]

    def weight(first, last):
        return weights[:, :, :, first:last].reshape(width, last - first)

    values[...] = jnp.dot(tokens[...], weight(0, width), preferred_element_type=f32)
    span = width // pool_heads
    head_of = lax.broadcasted_iota(jnp.int32, (latents * pool_heads, width), 1) // span
    row_of = lax.broadcasted_iota(jnp.int32, (latents * pool_heads, width), 0)
    pooled = []
    for m in range(latents):
        spread = jnp.where(row_of == head_of + m * pool_heads, 1.0, 0.0).astype(bf16)
        share = jnp.dot(mix[...], spread, preferred_element_type=f32) * values[...]
        pooled.append(jnp.sum(share.reshape(level_count, cells, width), axis=0).astype(bf16))
    pooled = jnp.concatenate(pooled, axis=0)
    latent = jnp.dot(pooled, weight(width, 2 * width), preferred_element_type=f32)
    base_rows = jnp.broadcast_to(base[...].astype(f32)[:, None, :], (latents, cells, width))
    latent = (latent + base_rows.reshape(latents * cells, width)).astype(bf16)

    full = latent.astype(f32)
    centred = full - jnp.mean(full, axis=-1, keepdims=True)
    variance = jnp.mean(centred * centred, axis=-1, keepdims=True)
    normed = (centred * lax.rsqrt(variance + STABILIZER_TINY) * gain[...]).astype(bf16)
    qkv = jnp.dot(normed, weight(2 * width, 5 * width), preferred_element_type=f32)
    qkv = qkv.astype(bf16)

    tokens_in = latents * cells
    quarter_labels = [labels[k : k + 1, 0:1] for k in range(4)]

    def labels_of(shape, axis):
        cell = lax.rem(lax.broadcasted_iota(jnp.int32, shape, axis), cells)
        label = jnp.full(shape, -1.0, jnp.float32)
        for k in range(3, -1, -1):
            label = jnp.where(
                cell < CELLS * (k + 1), jnp.broadcast_to(quarter_labels[k], shape), label
            )
        return label

    allowed = labels_of((tokens_in, 1), 0) == labels_of((1, tokens_in), 1)
    head_dim = width // heads
    pair = 2 * head_dim
    lane = lax.broadcasted_iota(jnp.int32, (1, pair), 1)
    left = jnp.where(lane < head_dim, 1.0, 0.0)
    scale = head_dim**-0.5
    sides = ((left * scale).astype(bf16), ((1.0 - left) * scale).astype(bf16))
    ones = jnp.ones((tokens_in, pair), bf16)
    attended = []
    for h in range(heads // 2):
        q = qkv[:, h * pair : (h + 1) * pair]
        k = qkv[:, width + h * pair : width + (h + 1) * pair]
        v = qkv[:, 2 * width + h * pair : 2 * width + (h + 1) * pair]
        v = jnp.concatenate([v, ones], axis=1)
        both = []
        for side in sides:
            logits = lax.dot_general(
                q * side, k, (((1,), (1,)), ((), ())), preferred_element_type=f32
            )
            logits = jnp.where(allowed, logits, -1e30)
            grown = jnp.exp(logits - jnp.max(logits, axis=-1, keepdims=True)).astype(bf16)
            both.append(jnp.dot(grown, v, preferred_element_type=f32))
        total = jnp.where(lane < head_dim, both[0][:, pair:], both[1][:, pair:])
        sums = jnp.where(lane < head_dim, both[0][:, :pair], both[1][:, :pair])
        attended.append((sums / total).astype(bf16))
    attended = jnp.concatenate(attended, axis=1)
    result = jnp.dot(attended, weight(5 * width, 6 * width), preferred_element_type=f32)
    result = full + result.astype(bf16).astype(f32)
    for k, out in enumerate((own, east, band, corner)):
        for m in range(latents):
            at = m * cells + k * CELLS
            out[m] = result[at : at + CELLS].astype(bf16)


def body(
    level_tokens,
    hidden_probe_match_matrix,
    value_weight,
    pool_out_weight,
    latent_base,
    norm_gain,
    qkv_weight,
    attn_out_weight,
    region_ids,
):
    levels, row_count, col_count, width = level_tokens.shape
    latents, pool_heads, _ = hidden_probe_match_matrix.shape
    lat_count, lon_count = lax.axis_size("lat"), lax.axis_size("lon")
    i, j = lax.axis_index("lat"), lax.axis_index("lon")
    odd = j % 2
    parity = (i // LAT_RING) % 2

    joined = jnp.concatenate([value_weight, pool_out_weight, qkv_weight, attn_out_weight], axis=1)
    piece_rows, all_columns = joined.shape
    half = all_columns // 2
    groups = lon_count // 2
    mine = lax.dynamic_slice(joined, (0, parity * half), (piece_rows, half))
    mine = jnp.broadcast_to(mine[None], (groups, piece_rows, half))
    same_core = [list(range(core, lon_count, 2)) for core in range(2)]
    mine = lax.all_to_all(mine, "lon", 0, 0, tiled=True, axis_index_groups=same_core)

    vmem = pl.BlockSpec(memory_space=pltpu.VMEM)
    smem = pl.BlockSpec(memory_space=pltpu.SMEM)
    window = jnp.where(odd == 0, i, (i + lat_count - 1) % lat_count)
    place = jnp.stack([parity, odd, (window == lat_count - 1).astype(jnp.int32)]).astype(jnp.int32)
    packed = levels * CELLS + 6
    quarter = jax.ShapeDtypeStruct((packed, width), level_tokens.dtype)
    own, east, band, corner = pl.pallas_call(
        quarter_kernel,
        out_shape=[quarter] * 4,
        in_specs=[smem, smem, vmem],
        out_specs=[vmem] * 4,
        scratch_shapes=[pltpu.VMEM((packed, width), jnp.float32)],
        compiler_params=pltpu.CompilerParams(vmem_limit_bytes=LIMIT),
        name="quarters",
    )(place, region_ids, jnp.transpose(level_tokens, (1, 2, 0, 3)))
    band = fetch(band, along)
    corner = fetch(corner, across)
    mine, band, corner, east = lax.optimization_barrier((mine, band, corner, east))
    ahead = fetch(mine, next_along_x)
    east = fetch(east, beside)

    mine_swapped = fetch(mine, other_core)
    ahead, east = lax.optimization_barrier((ahead, east))
    token_rows = levels * PADDED
    mixes = latents * pool_heads
    tokens, mix, labels = pl.pallas_call(
        functools.partial(mix_kernel, levels),
        out_shape=[
            jax.ShapeDtypeStruct((token_rows, width), jnp.bfloat16),
            jax.ShapeDtypeStruct((token_rows, mixes), jnp.bfloat16),
            jax.ShapeDtypeStruct((8, 128), jnp.float32),
        ],
        in_specs=[smem] + [vmem] * 5,
        out_specs=[vmem] * 3,
        scratch_shapes=[
            pltpu.VMEM((width // 128, packed, 128), jnp.float32),
            pltpu.VMEM((levels, PADDED, width), jnp.float32),
        ],
        compiler_params=pltpu.CompilerParams(vmem_limit_bytes=LIMIT),
        cost_estimate=pl.CostEstimate(
            flops=2 * token_rows * width * mixes, bytes_accessed=8 << 20, transcendentals=0
        ),
        name="mix",
    )(place, own, east, band, corner, hidden_probe_match_matrix.reshape(mixes, width))

    ahead_swapped = fetch(ahead, other_core)
    out = pl.pallas_call(
        functools.partial(window_kernel, HEADS, pool_heads),
        out_shape=[jax.ShapeDtypeStruct((latents, CELLS, width), jnp.bfloat16)] * 4,
        in_specs=[smem] + [vmem] * 9,
        out_specs=[vmem] * 4,
        scratch_shapes=[
            pltpu.VMEM((groups, 2, piece_rows, all_columns), jnp.bfloat16),
            pltpu.VMEM((token_rows, width), jnp.float32),
        ],
        compiler_params=pltpu.CompilerParams(vmem_limit_bytes=LIMIT),
        name="window",
    )(
        place,
        tokens,
        mix,
        mine,
        ahead,
        mine_swapped,
        ahead_swapped,
        labels,
        latent_base,
        norm_gain.reshape(1, width),
    )

    def part_of(k):
        return out[k].reshape(latents, HALF_LAT, HALF_LON, width)

    to_band = give_back(part_of(2), along)
    to_corner = give_back(part_of(3), across)
    to_east = give_back(part_of(1), beside)
    kept_rows = jnp.concatenate([to_corner, part_of(0)], axis=2)
    other_rows = jnp.concatenate([to_east, to_band], axis=2)
    return jnp.where(
        odd == 0,
        jnp.concatenate([other_rows, kept_rows], axis=1),
        jnp.concatenate([kept_rows, other_rows], axis=1),
    )


def solution(mesh):
    placed = (
        P(None, "lat", "lon", None),
        P(),
        P("lon", None),
        P("lon", None),
        P(),
        P(),
        P("lon", None),
        P("lon", None),
        P("lat", "lon"),
    )
    return jax.shard_map(
        body, mesh=mesh, in_specs=placed, out_specs=P(None, "lat", "lon", None), check_vma=False
    )
```
